32 devices in a mesh: parts: 2 (over y), blk: 16 (over z, x, core).
Axes of the slice: x: 2, y: 2, z: 4, core: 2. Of those that a mesh axis runs over, the one named last changes fastest.
Arguments:
- codes: bfloat16 [8192, 1024], P(('parts', 'blk')), parts along dimension 0, may hold values from -8 to 8
- exponents: int32 [8192, 32], P(('parts', 'blk')), parts along dimension 0, may hold values from -2 to 2
- clusters: int32 [8192], P(('parts', 'blk')), parts along dimension 0, may hold values from 0 to 63, as said below
Outputs:
- best: float32 [8192], P(('parts', 'blk')), parts along dimension 0
The draws below stay inside these ranges and needn't reach their ends.
There are 2 independent parts, one for each index of `parts`. The reference program is written for one: setup_inputs(seed, part) draws one part's arguments, and reference() takes and returns one part's arrays. A program takes and returns all parts, laid end to end along the dimension named above; each array names one. Nothing has to cross between parts.
Inputs may be any that keep to these rules, and one draw needn't show every extreme that they name: The owner of a cluster is cluster // 4. Among the rows of one device, at most 48 have clusters of one owner, and every device has exactly 48 rows of some owner.
All inputs are finite; a program needn't handle non-finite values.
Results may differ from the reference program's by a relative error of at most 0.0003.
Values may be sent and summed in bfloat16 or wider, within the bound.
No kernel may reach another device: no remote copies, remote signals or barrier semaphores. Data moves between devices by JAX's collectives and lax.ppermute only.
A program may use at most 64 MiB of HBM per device.

```python
import math
import jax
import jax.numpy as jnp
from jax import lax

E = 1024
GROUP = 32
GROUPS = 32
ROWS_DEV = 256
CL_DEV = 4
CAP = 48
CLUSTERS = 64
ROWS = 4096
N_BLK = 16


def routing(key):
    heat = jax.random.randint(jax.random.fold_in(key, 5), (N_BLK,), 0, 6)
    device_keys = jax.random.split(jax.random.fold_in(key, 6), N_BLK)
    slots = jnp.arange(N_BLK * CAP, dtype=jnp.int32)
    owner = slots // CAP

    def one_device(device_key, forced):
        first, second, third = jax.random.split(device_key, 3)
        priority = jax.random.randint(first, (N_BLK * CAP,), 0, 4096) + heat[owner] * 1024 + jnp.where(owner == forced, 16384, 0)
        priority = priority * (N_BLK * CAP) + slots
        chosen = lax.top_k(priority, ROWS_DEV)[1].astype(jnp.int32)
        chosen = chosen[jax.random.permutation(second, ROWS_DEV)]
        chosen_owner = chosen // CAP
        within = jnp.where(chosen_owner == forced, chosen % CAP % CL_DEV, jax.random.randint(third, (ROWS_DEV,), 0, CL_DEV))
        return chosen_owner * CL_DEV + within
    return jax.vmap(one_device)(device_keys, jnp.arange(N_BLK, dtype=jnp.int32)).reshape(ROWS)


def draw_clusters(key, part):
    return routing(key)


def draw_codes(key, part):
    members = routing(key)
    key = jax.random.fold_in(key, 21)
    centre_key, noise_key = jax.random.split(key)
    centres = jax.random.normal(centre_key, (CLUSTERS, E), jnp.float32)
    noise = jax.random.normal(noise_key, (ROWS, E), jnp.float32)
    return jnp.clip(centres[members] + noise, -8.0, 8.0).astype(jnp.bfloat16)


def place_ends(drawn, key, least, high):
    spot = [jax.random.randint(jax.random.fold_in(key, axis), (), 0, length) for axis, length in enumerate(drawn.shape)]
    longest = drawn.shape.index(max(drawn.shape))
    neighbour = spot[:longest] + [(spot[longest] + 1) % drawn.shape[longest]] + spot[longest + 1:]
    return drawn.at[tuple(spot)].set(least).at[tuple(neighbour)].set(high)


def setup_inputs(seed: int = 0, part: int = 0) -> dict:
    keys = jax.random.split(jax.random.key(seed), 4)
    own_keys = jax.random.split(jax.random.fold_in(keys[3], part), 4)
    return {
        "codes": draw_codes(jax.random.fold_in(jax.random.fold_in(keys[3], part), 71), part),
        "exponents": place_ends(jax.random.randint(own_keys[1], (ROWS, GROUPS), -2, 3), jax.random.fold_in(own_keys[1], 1), -2, 2).astype(jnp.int32),
        "clusters": draw_clusters(jax.random.fold_in(jax.random.fold_in(keys[3], part), 71), part),
    }


def dequantize(codes, exponents):
    rows = codes.shape[0]
    grouped = codes.astype(jnp.float32).reshape(rows, -1, GROUP) * jnp.exp2(exponents.astype(jnp.float32))[:, :, None]
    return grouped.reshape(rows, -1).astype(jnp.bfloat16)

def inverse_norm(values):
    wide = values.astype(jnp.float32)
    return lax.rsqrt(lax.optimization_barrier(jnp.sum(wide * wide, axis=1)) + 1e-06)

def similarity(left, left_inverse, right, right_inverse):
    dots = lax.dot_general(left, right, (((1,), (1,)), ((), ())), preferred_element_type=jnp.float32)
    return dots * left_inverse[:, None] * right_inverse[None, :]

def reference(codes, exponents, clusters):
    values = dequantize(codes, exponents)
    inverse = inverse_norm(values)
    total = codes.shape[0]
    block_rows = math.gcd(total, 512)
    identity = jnp.arange(total, dtype=jnp.int32)

    def block_best(start):
        part = lax.dynamic_slice_in_dim(values, start, block_rows, 0)
        part_inverse = lax.dynamic_slice_in_dim(inverse, start, block_rows, 0)
        part_clusters = lax.dynamic_slice_in_dim(clusters, start, block_rows, 0)
        part_index = lax.dynamic_slice_in_dim(identity, start, block_rows, 0)
        scores = similarity(part, part_inverse, values, inverse)
        same = (part_clusters[:, None] == clusters[None, :]) & (part_index[:, None] != identity[None, :])
        return lax.optimization_barrier(jnp.max(jnp.where(same, scores, -1.0), axis=1))
    starts = jnp.arange(total // block_rows, dtype=jnp.int32) * block_rows
    return lax.map(block_best, starts).reshape(total)
```

```python
import functools
import jax
import jax.numpy as jnp
from jax import lax
from jax.experimental import pallas as pl
from jax.experimental.pallas import tpu as pltpu
from jax.sharding import PartitionSpec as P

GROUP = 32
META_ROWS = 40
VMEM_LIMIT = 32 * 1024 * 1024


def expand(lane_row, rows):
    eye = lax.broadcasted_iota(jnp.int32, (rows, rows), 0) == lax.broadcasted_iota(jnp.int32, (rows, rows), 1)
    return jnp.sum(jnp.where(eye, lane_row, 0.0), axis=1, keepdims=True)


def flatten(column, rows):
    eye = lax.broadcasted_iota(jnp.int32, (rows, rows), 0) == lax.broadcasted_iota(jnp.int32, (rows, rows), 1)
    return jnp.sum(jnp.where(eye, column, 0.0), axis=0, keepdims=True)


def dequantize(codes, meta, groups):
    width = codes.shape[1]
    spread = (
        lax.broadcasted_iota(jnp.int32, (groups, width), 1) // GROUP
        == lax.broadcasted_iota(jnp.int32, (groups, width), 0)
    ).astype(jnp.bfloat16)
    scale = lax.dot_general(
        meta[:groups].astype(jnp.bfloat16), spread, (((0,), (0,)), ((), ())),
        preferred_element_type=jnp.float32,
    )
    values = (codes.astype(jnp.float32) * scale).astype(jnp.bfloat16)
    wide = values.astype(jnp.float32)
    inverse = lax.rsqrt(jnp.sum(wide * wide, axis=1, keepdims=True) + 1e-06)
    return values, inverse, meta[groups:groups + 1]


def plane_kernel(planes, groups, *refs):
    code_refs, meta_refs = refs[:planes], refs[planes:2 * planes]
    values_ref, side_ref, best_ref = refs[2 * planes:]
    rows = code_refs[0].shape[0]
    own = own_inverse = own_code = None
    best = jnp.full((1, rows), -1.0, jnp.float32)
    for r in range(planes):
        values, inverse, code = dequantize(code_refs[r][...], meta_refs[r][...], groups)
        values_ref[r * rows:(r + 1) * rows] = values
        inverse_row = flatten(inverse, rows)
        side_ref[0:1, r * rows:(r + 1) * rows] = code
        side_ref[1:2, r * rows:(r + 1) * rows] = inverse_row
        if r == 0:
            own, own_inverse, own_code = values, inverse_row, code
        dots = lax.dot_general(
            values, own, (((1,), (1,)), ((), ())), preferred_element_type=jnp.float32
        )
        same = expand(code, rows) == own_code
        if r == 0:
            same &= (
                lax.broadcasted_iota(jnp.int32, (rows, rows), 0)
                != lax.broadcasted_iota(jnp.int32, (rows, rows), 1)
            )
        scores = jnp.where(same, dots * inverse * own_inverse, -1.0)
        best = jnp.maximum(best, jnp.max(scores, axis=0, keepdims=True))
    best_ref[...] = jnp.full(best_ref.shape, -1.0, jnp.float32)
    best_ref[0:1, 0:rows] = best


def block_kernel(planes, groups, codes_ref, meta_ref, values_ref, side_ref, before_ref, best_ref, back_ref):
    rows = codes_ref.shape[0]
    values, inverse, code = dequantize(codes_ref[...], meta_ref[...], groups)
    code = expand(code, rows)
    back = jnp.full((rows, 1), -1.0, jnp.float32)
    for r in range(planes):
        at = slice(r * rows, (r + 1) * rows)
        dots = lax.dot_general(
            values, values_ref[at], (((1,), (1,)), ((), ())), preferred_element_type=jnp.float32
        )
        same = code == side_ref[0:1, at]
        scores = jnp.where(same, dots * inverse * side_ref[1:2, at], -1.0)
        back = jnp.maximum(back, jnp.max(scores, axis=1, keepdims=True))
        best_ref[0:1, at] = jnp.maximum(before_ref[0:1, at], jnp.max(scores, axis=0, keepdims=True))
    back_ref[...] = flatten(back, rows)


def call(kernel, shapes, flops, *operands):
    spec = pl.BlockSpec(memory_space=pltpu.VMEM)
    return pl.pallas_call(
        kernel,
        out_shape=[jax.ShapeDtypeStruct(shape, dtype) for shape, dtype in shapes],
        in_specs=[spec] * len(operands),
        out_specs=[spec] * len(shapes),
        compiler_params=pltpu.CompilerParams(vmem_limit_bytes=VMEM_LIMIT),
        cost_estimate=pl.CostEstimate(flops=flops, bytes_accessed=4 * 1024 * 1024, transcendentals=0),
    )(*operands)


def split_axis(count):
    planes = 1
    while planes * planes * 4 <= count:
        planes *= 2
    if count % planes or (count // planes) & (count // planes - 1):
        return 1, count
    return planes, count // planes


def far_rounds(height):
    rounds = []
    for step in range(2, height, 2):
        top = 1 << (step.bit_length() - 1)
        rounds.append([(a, a ^ (step + 1) if a & top else a ^ step) for a in range(height)])
    if height > 1:
        rounds.append([(a, a ^ 1) for a in range(height) if (a & 1) != (a >> 1 & 1)])
    return rounds


def shards(codes, exponents, clusters):
    count = lax.axis_size("blk")
    rows, width = codes.shape
    groups = exponents.shape[1]
    plane, height = split_axis(count)
    near = [
        [(z * plane + p, z * plane + (p ^ r)) for z in range(height) for p in range(plane)]
        for r in range(plane)
    ]
    far = [
        [(a * plane + p, b * plane + p) for a, b in pairs for p in range(plane)]
        for pairs in far_rounds(height)
    ]
    meta = jnp.concatenate(
        [
            jnp.exp2(exponents.astype(jnp.float32)).T,
            (clusters + 1).astype(jnp.float32)[None],
            jnp.zeros((META_ROWS - groups - 1, rows), jnp.float32),
        ]
    )
    far_codes = [lax.ppermute(codes, "blk", pairs) for pairs in far]
    far_meta = [lax.ppermute(meta, "blk", pairs) for pairs in far]
    near_codes = [codes] + [lax.ppermute(codes, "blk", pairs) for pairs in near[1:]]
    near_meta = [meta] + [lax.ppermute(meta, "blk", pairs) for pairs in near[1:]]

    block_flops = 2 * rows * rows * width * plane
    values, side, best = call(
        functools.partial(plane_kernel, plane, groups),
        [
            ((plane * rows, width), jnp.bfloat16),
            ((8, plane * rows), jnp.float32),
            ((1, plane * rows), jnp.float32),
        ],
        block_flops, *near_codes, *near_meta,
    )
    backs = []
    for far_code, far_side in reversed(list(zip(far_codes, far_meta))):
        best, back = call(
            functools.partial(block_kernel, plane, groups),
            [((1, plane * rows), jnp.float32), ((1, rows), jnp.float32)],
            block_flops, far_code, far_side, values, side, best,
        )
        backs.append(back)
    backs.reverse()

    result = best[:, :rows]
    for r in range(1, plane):
        result = jnp.maximum(
            result, lax.ppermute(best[:, r * rows:(r + 1) * rows], "blk", near[r])
        )
    me = lax.axis_index("blk")
    for pairs, back in zip(far, backs):
        home = lax.ppermute(back, "blk", [(b, a) for a, b in pairs])
        if len(pairs) < count:
            sent = functools.reduce(jnp.logical_or, [me == a for a, _ in pairs])
            home = jnp.where(sent, home, -1.0)
        result = jnp.maximum(result, home)
    return result.reshape(rows)


def solution(mesh):
    placed = (P(("parts", "blk"), None), P(("parts", "blk"), None), P(("parts", "blk")))
    return jax.shard_map(
        shards, mesh=mesh, in_specs=placed, out_specs=P(("parts", "blk")), check_vma=False
    )
```

```python
import functools
import jax
import jax.numpy as jnp
from jax import lax
from jax.experimental import pallas as pl
from jax.experimental.pallas import tpu as pltpu
from jax.sharding import PartitionSpec as P

GROUP = 32
SIDE_ROWS = 16
COST = 1
VMEM_LIMIT = 32 * 1024 * 1024


def expand(lane_row, rows):
    eye = lax.broadcasted_iota(jnp.int32, (rows, rows), 0) == lax.broadcasted_iota(jnp.int32, (rows, rows), 1)
    return jnp.sum(jnp.where(eye, lane_row, 0.0), axis=1, keepdims=True)


def flatten(column, rows):
    eye = lax.broadcasted_iota(jnp.int32, (rows, rows), 0) == lax.broadcasted_iota(jnp.int32, (rows, rows), 1)
    return jnp.sum(jnp.where(eye, column, 0.0), axis=0, keepdims=True)


def pack_kernel(groups, codes_hbm, exponents_hbm, clusters_hbm, message_ref, codes_ref, exponents_ref, clusters_ref, sems):
    copies = [
        pltpu.make_async_copy(source, target, sems.at[i])
        for i, (source, target) in enumerate(
            [(exponents_hbm, exponents_ref), (clusters_hbm, clusters_ref), (codes_hbm, codes_ref)]
        )
    ]
    for copy in copies:
        copy.start()
    rows, width = codes_ref.shape
    copies[1].wait()
    code = clusters_ref[...] + 1
    row = lax.broadcasted_iota(jnp.int32, (SIDE_ROWS, rows), 0)
    side = jnp.where(row == 0, code >> 8, jnp.where(row == 1, code & 255, 0))
    message_ref[rows:, 0:rows] = side.astype(jnp.float32).astype(jnp.bfloat16)
    message_ref[rows:, rows:] = jnp.zeros((SIDE_ROWS, width - rows), jnp.bfloat16)
    spread = (
        lax.broadcasted_iota(jnp.int32, (groups, width), 1) // GROUP
        == lax.broadcasted_iota(jnp.int32, (groups, width), 0)
    ).astype(jnp.bfloat16)
    copies[0].wait()
    scale = lax.dot_general(
        jnp.exp2(exponents_ref[...].astype(jnp.float32)).astype(jnp.bfloat16), spread,
        (((0,), (0,)), ((), ())), preferred_element_type=jnp.float32,
    )
    copies[2].wait()
    message_ref[0:rows] = (codes_ref[...].astype(jnp.float32) * scale).astype(jnp.bfloat16)


def unpack(message_ref):
    rows = message_ref.shape[0] - SIDE_ROWS
    values = message_ref[0:rows]
    wide = values.astype(jnp.float32)
    inverse = lax.rsqrt(jnp.sum(wide * wide, axis=1, keepdims=True) + 1e-06)
    side = message_ref[rows:, 0:rows].astype(jnp.float32)
    return values, inverse, side[0:1] * 256.0 + side[1:2]


def plane_kernel(planes, *refs):
    side_ref, best_ref = refs[planes:]
    rows = refs[0].shape[0] - SIDE_ROWS
    best = jnp.full((1, rows), -1.0, jnp.float32)
    for r in range(planes):
        values, inverse, code = unpack(refs[r])
        inverse_row = flatten(inverse, rows)
        side_ref[0:1, r * rows:(r + 1) * rows] = code
        side_ref[1:2, r * rows:(r + 1) * rows] = inverse_row
        if r == 0:
            own, own_inverse, own_code = values, inverse_row, code
        dots = lax.dot_general(
            values, own, (((1,), (1,)), ((), ())), preferred_element_type=jnp.float32
        )
        same = expand(code, rows) == own_code
        if r == 0:
            same &= (
                lax.broadcasted_iota(jnp.int32, (rows, rows), 0)
                != lax.broadcasted_iota(jnp.int32, (rows, rows), 1)
            )
        scores = jnp.where(same, dots * inverse * own_inverse, -1.0)
        best = jnp.maximum(best, jnp.max(scores, axis=0, keepdims=True))
    best_ref[...] = jnp.full(best_ref.shape, -1.0, jnp.float32)
    best_ref[0:1, 0:rows] = best


def block_kernel(planes, *refs):
    block_ref, near_refs = refs[0], refs[1:1 + planes]
    side_ref, before_ref, best_ref, back_ref = refs[1 + planes:]
    values, inverse, code = unpack(block_ref)
    rows = values.shape[0]
    code = expand(code, rows)
    back = jnp.full((rows, 1), -1.0, jnp.float32)
    for r in range(planes):
        at = slice(r * rows, (r + 1) * rows)
        dots = lax.dot_general(
            values, near_refs[r][0:rows], (((1,), (1,)), ((), ())),
            preferred_element_type=jnp.float32,
        )
        same = code == side_ref[0:1, at]
        scores = jnp.where(same, dots * inverse * side_ref[1:2, at], -1.0)
        back = jnp.maximum(back, jnp.max(scores, axis=1, keepdims=True))
        best_ref[0:1, at] = jnp.maximum(before_ref[0:1, at], jnp.max(scores, axis=0, keepdims=True))
    back_ref[...] = flatten(back, rows)


def call(kernel, shapes, *operands):
    spec = pl.BlockSpec(memory_space=pltpu.VMEM)
    return pl.pallas_call(
        kernel,
        out_shape=[jax.ShapeDtypeStruct(shape, dtype) for shape, dtype in shapes],
        in_specs=[spec] * len(operands),
        out_specs=[spec] * len(shapes),
        compiler_params=pltpu.CompilerParams(vmem_limit_bytes=VMEM_LIMIT),
        cost_estimate=pl.CostEstimate(flops=COST, bytes_accessed=1, transcendentals=0),
    )(*operands)


def split_axis(count):
    planes = 1
    while planes * planes * 4 <= count:
        planes *= 2
    if count % planes or (count // planes) & (count // planes - 1):
        return 1, count
    return planes, count // planes


def far_rounds(height):
    rounds = []
    for step in range(2, height, 2):
        top = 1 << (step.bit_length() - 1)
        rounds.append([(a, a ^ (step + 1) if a & top else a ^ step) for a in range(height)])
    if height > 1:
        rounds.append([(a, a ^ 1) for a in range(height) if (a & 1) != (a >> 1 & 1)])
    return rounds


def shards(codes, exponents, clusters):
    count = lax.axis_size("blk")
    rows, width = codes.shape
    groups = exponents.shape[1]
    plane, height = split_axis(count)
    near = [
        [(z * plane + p, z * plane + (p ^ r)) for z in range(height) for p in range(plane)]
        for r in range(plane)
    ]
    far = [
        [(a * plane + p, b * plane + p) for a, b in pairs for p in range(plane)]
        for pairs in far_rounds(height)
    ]
    message = pl.pallas_call(
        functools.partial(pack_kernel, groups),
        out_shape=jax.ShapeDtypeStruct((rows + SIDE_ROWS, width), jnp.bfloat16),
        in_specs=[pl.BlockSpec(memory_space=pl.ANY)] * 3,
        out_specs=pl.BlockSpec(memory_space=pltpu.VMEM),
        scratch_shapes=[
            pltpu.VMEM((rows, width), jnp.bfloat16),
            pltpu.VMEM((groups, rows), jnp.int32),
            pltpu.VMEM((1, rows), jnp.int32),
            pltpu.SemaphoreType.DMA((3,)),
        ],
        compiler_params=pltpu.CompilerParams(vmem_limit_bytes=VMEM_LIMIT),
    )(codes, exponents.T, clusters[None])
    far_blocks = [lax.ppermute(message, "blk", pairs) for pairs in far]
    near_blocks = [message] + [lax.ppermute(message, "blk", pairs) for pairs in near[1:]]
    side, best = call(
        functools.partial(plane_kernel, plane),
        [((8, plane * rows), jnp.float32), ((1, plane * rows), jnp.float32)],
        *near_blocks,
    )
    backs = []
    for block in reversed(far_blocks):
        best, back = call(
            functools.partial(block_kernel, plane),
            [((1, plane * rows), jnp.float32), ((1, rows), jnp.float32)],
            block, *near_blocks, side, best,
        )
        backs.append(back)
    backs.reverse()

    result = best[:, :rows]
    for r in range(1, plane):
        result = jnp.maximum(
            result, lax.ppermute(best[:, r * rows:(r + 1) * rows], "blk", near[r])
        )
    me = lax.axis_index("blk")
    for pairs, back in zip(far, backs):
        home = lax.ppermute(back, "blk", [(b, a) for a, b in pairs])
        if len(pairs) < count:
            sent = functools.reduce(jnp.logical_or, [me == a for a, _ in pairs])
            home = jnp.where(sent, home, -1.0)
        result = jnp.maximum(result, home)
    return result.reshape(rows)


def solution(mesh):
    placed = (P(("parts", "blk"), None), P(("parts", "blk"), None), P(("parts", "blk")))
    return jax.shard_map(
        shards, mesh=mesh, in_specs=placed, out_specs=P(("parts", "blk")), check_vma=False
    )
```

```python
import functools
import jax
import jax.numpy as jnp
from jax import lax
from jax.experimental import pallas as pl
from jax.experimental.pallas import tpu as pltpu
from jax.sharding import PartitionSpec as P

GROUP = 32
SIDE_ROWS = 16
COST = 1
CHUNKS = 4
PACK_LIMIT = 32 * 1024 * 1024
VMEM_LIMIT = 32 * 1024 * 1024


def expand(lane_row, rows):
    eye = lax.broadcasted_iota(jnp.int32, (rows, rows), 0) == lax.broadcasted_iota(jnp.int32, (rows, rows), 1)
    return jnp.sum(jnp.where(eye, lane_row, 0.0), axis=1, keepdims=True)


def flatten(column, rows):
    eye = lax.broadcasted_iota(jnp.int32, (rows, rows), 0) == lax.broadcasted_iota(jnp.int32, (rows, rows), 1)
    return jnp.sum(jnp.where(eye, column, 0.0), axis=0, keepdims=True)


def spread_scale(scale, width):
    groups = scale.shape[0]
    spread = (
        lax.broadcasted_iota(jnp.int32, (groups, width), 1) // GROUP
        == lax.broadcasted_iota(jnp.int32, (groups, width), 0)
    ).astype(jnp.bfloat16)
    return lax.dot_general(
        scale, spread, (((0,), (0,)), ((), ())), preferred_element_type=jnp.float32
    )


def pack_kernel(groups, codes_hbm, exponents_hbm, clusters_hbm, message_ref, side_ref, codes_ref, exponents_ref, clusters_ref, sems):
    copies = [
        pltpu.make_async_copy(source, target, sems.at[i])
        for i, (source, target) in enumerate(
            [(exponents_hbm, exponents_ref), (clusters_hbm, clusters_ref), (codes_hbm, codes_ref)]
        )
    ]
    for copy in copies:
        copy.start()
    rows, width = codes_ref.shape
    copies[1].wait()
    code = clusters_ref[...] + 1
    row = lax.broadcasted_iota(jnp.int32, (SIDE_ROWS, rows), 0)
    side = jnp.where(row == 0, code >> 8, jnp.where(row == 1, code & 255, 0))
    side = side.astype(jnp.float32).astype(jnp.bfloat16)
    message_ref[rows:, 0:rows] = side
    message_ref[rows:, rows:] = jnp.zeros((SIDE_ROWS, width - rows), jnp.bfloat16)
    side_ref[groups:] = side
    copies[0].wait()
    scale = jnp.exp2(exponents_ref[...].astype(jnp.float32)).astype(jnp.bfloat16)
    side_ref[0:groups] = scale
    scale = spread_scale(scale, width)
    copies[2].wait()
    message_ref[0:rows] = (codes_ref[...].astype(jnp.float32) * scale).astype(jnp.bfloat16)


def cluster_code(parts):
    parts = parts.astype(jnp.float32)
    return parts[0:1] * 256.0 + parts[1:2]


def inverse_norm(values):
    wide = values.astype(jnp.float32)
    return lax.rsqrt(jnp.sum(wide * wide, axis=1, keepdims=True) + 1e-06)


def unpack_near(message_ref):
    rows = message_ref.shape[0] - SIDE_ROWS
    values = message_ref[0:rows]
    return values, inverse_norm(values), cluster_code(message_ref[rows:, 0:rows])


def unpack_far(codes_ref, side_ref):
    groups = side_ref.shape[0] - SIDE_ROWS
    scale = spread_scale(side_ref[0:groups], codes_ref.shape[1])
    values = (codes_ref[...].astype(jnp.float32) * scale).astype(jnp.bfloat16)
    return values, inverse_norm(values), cluster_code(side_ref[groups:])


def plane_kernel(planes, *refs):
    values_ref, lanes_ref, best_ref = refs[planes:]
    rows = refs[0].shape[0] - SIDE_ROWS
    best = jnp.full((1, rows), -1.0, jnp.float32)
    for r in range(planes):
        values, inverse, code = unpack_near(refs[r])
        values_ref[r * rows:(r + 1) * rows] = values
        inverse_row = flatten(inverse, rows)
        lanes_ref[0:1, r * rows:(r + 1) * rows] = code
        lanes_ref[1:2, r * rows:(r + 1) * rows] = inverse_row
        if r == 0:
            own, own_inverse, own_code = values, inverse_row, code
        dots = lax.dot_general(
            values, own, (((1,), (1,)), ((), ())), preferred_element_type=jnp.float32
        )
        same = expand(code, rows) == own_code
        if r == 0:
            same &= (
                lax.broadcasted_iota(jnp.int32, (rows, rows), 0)
                != lax.broadcasted_iota(jnp.int32, (rows, rows), 1)
            )
        scores = jnp.where(same, dots * inverse * own_inverse, -1.0)
        best = jnp.maximum(best, jnp.max(scores, axis=0, keepdims=True))
    best_ref[...] = jnp.full(best_ref.shape, -1.0, jnp.float32)
    best_ref[0:1, 0:rows] = best


def far_kernel(planes, fars, *refs):
    code_refs, side_refs = refs[:fars], refs[fars:2 * fars]
    values_ref, lanes_ref, before_ref = refs[2 * fars:2 * fars + 3]
    outs = refs[2 * fars + 3:]
    back_refs, best_refs = outs[:fars], outs[fars:]
    rows = code_refs[0].shape[0]
    bests = [before_ref[0:1, r * rows:(r + 1) * rows] for r in range(planes)]
    for code_ref, side_ref, back_ref in zip(code_refs, side_refs, back_refs):
        values, inverse, code = unpack_far(code_ref, side_ref)
        code = expand(code, rows)
        back = jnp.full((rows, 1), -1.0, jnp.float32)
        for r in range(planes):
            at = slice(r * rows, (r + 1) * rows)
            dots = lax.dot_general(
                values, values_ref[at], (((1,), (1,)), ((), ())),
                preferred_element_type=jnp.float32,
            )
            same = code == lanes_ref[0:1, at]
            scores = jnp.where(same, dots * inverse * lanes_ref[1:2, at], -1.0)
            back = jnp.maximum(back, jnp.max(scores, axis=1, keepdims=True))
            bests[r] = jnp.maximum(bests[r], jnp.max(scores, axis=0, keepdims=True))
        back_ref[...] = flatten(back, rows)
    for r in range(planes):
        best_refs[r][...] = bests[r]


def call(kernel, shapes, *operands):
    spec = pl.BlockSpec(memory_space=pltpu.VMEM)
    return pl.pallas_call(
        kernel,
        out_shape=[jax.ShapeDtypeStruct(shape, dtype) for shape, dtype in shapes],
        in_specs=[spec] * len(operands),
        out_specs=[spec] * len(shapes),
        compiler_params=pltpu.CompilerParams(vmem_limit_bytes=VMEM_LIMIT),
        cost_estimate=pl.CostEstimate(flops=COST, bytes_accessed=1, transcendentals=0),
    )(*operands)


def split_axis(count):
    planes = 1
    while planes * planes * 4 <= count:
        planes *= 2
    if count % planes or (count // planes) & (count // planes - 1):
        return 1, count
    return planes, count // planes


def far_rounds(height):
    rounds = []
    for step in range(2, height, 2):
        top = 1 << (step.bit_length() - 1)
        rounds.append([(a, a ^ (step + 1) if a & top else a ^ step) for a in range(height)])
    if height > 1:
        rounds.append([(a, a ^ 1) for a in range(height) if (a & 1) != (a >> 1 & 1)])
    return rounds


def shards(codes, exponents, clusters):
    count = lax.axis_size("blk")
    rows, width = codes.shape
    groups = exponents.shape[1]
    plane, height = split_axis(count)
    near = [
        [(z * plane + p, z * plane + (p ^ r)) for z in range(height) for p in range(plane)]
        for r in range(plane)
    ]
    far = [
        [(a * plane + p, b * plane + p) for a, b in pairs for p in range(plane)]
        for pairs in far_rounds(height)
    ]
    far_codes = [lax.ppermute(codes, "blk", pairs) for pairs in far]

    def near_phase(codes, exponents, clusters):
        message, side = pl.pallas_call(
            functools.partial(pack_kernel, groups),
            out_shape=[
                jax.ShapeDtypeStruct((rows + SIDE_ROWS, width), jnp.bfloat16),
                jax.ShapeDtypeStruct((groups + SIDE_ROWS, rows), jnp.bfloat16),
            ],
            in_specs=[pl.BlockSpec(memory_space=pl.ANY)] * 3,
            out_specs=[pl.BlockSpec(memory_space=pltpu.VMEM)] * 2,
            scratch_shapes=[
                pltpu.VMEM((rows, width), jnp.bfloat16),
                pltpu.VMEM((groups, rows), jnp.int32),
                pltpu.VMEM((1, rows), jnp.int32),
                pltpu.SemaphoreType.DMA((3,)),
            ],
            compiler_params=pltpu.CompilerParams(vmem_limit_bytes=PACK_LIMIT),
        )(codes, exponents, clusters)
        blocks = [message]
        for r in range(1, plane):
            relayed = r > 1 and r & 1
            blocks.append(
                lax.ppermute(blocks[r - 1], "blk", near[1]) if relayed
                else lax.ppermute(message, "blk", near[r])
            )
        if plane > 1:
            side, blocks[1] = lax.optimization_barrier((side, blocks[1]))
        sides = tuple(lax.ppermute(side, "blk", pairs) for pairs in far)
        values, lanes, best = call(
            functools.partial(plane_kernel, plane),
            [
                ((plane * rows, width), jnp.bfloat16),
                ((8, plane * rows), jnp.float32),
                ((1, plane * rows), jnp.float32),
            ],
            *blocks,
        )
        return values, sides, lanes, best

    values, far_sides, lanes, best = lax.cond(
        lax.axis_index("blk") >= 0,
        near_phase,
        lambda *operands: jax.tree.map(lambda t: jnp.zeros(t.shape, t.dtype), jax.eval_shape(near_phase, *operands)),
        codes, exponents.T, clusters[None],
    )
    outs = call(
        functools.partial(far_kernel, plane, len(far)),
        [((1, rows), jnp.float32)] * (plane + len(far)),
        *far_codes, *far_sides, values, lanes, best,
    )
    backs, bests = outs[:len(far)], outs[len(far):]

    homes = []
    me = lax.axis_index("blk")
    for pairs, back in reversed(list(zip(far, backs))):
        home = lax.ppermute(back, "blk", [(b, a) for a, b in pairs])
        if len(pairs) < count:
            sent = functools.reduce(jnp.logical_or, [me == a for a, _ in pairs])
            home = jnp.where(sent, home, -1.0)
        homes.append(home)
    for r in range(1, plane):
        homes.append(lax.ppermute(bests[r], "blk", near[r]))
    result = functools.reduce(jnp.maximum, homes, bests[0])
    return result.reshape(rows)


def solution(mesh):
    placed = (P(("parts", "blk"), None), P(("parts", "blk"), None), P(("parts", "blk")))
    return jax.shard_map(
        shards, mesh=mesh, in_specs=placed, out_specs=P(("parts", "blk")), check_vma=False
    )
```

```python
import functools
import jax
import jax.numpy as jnp
from jax import lax
from jax.experimental import pallas as pl
from jax.experimental.pallas import tpu as pltpu
from jax.sharding import PartitionSpec as P

GROUP = 32
SIDE_ROWS = 16
COST = 1
CHUNKS = 4
PACK_LIMIT = 32 * 1024 * 1024
VMEM_LIMIT = 32 * 1024 * 1024


def expand(lane_row, rows):
    eye = lax.broadcasted_iota(jnp.int32, (rows, rows), 0) == lax.broadcasted_iota(jnp.int32, (rows, rows), 1)
    return jnp.sum(jnp.where(eye, lane_row, 0.0), axis=1, keepdims=True)


def flatten(column, rows):
    eye = lax.broadcasted_iota(jnp.int32, (rows, rows), 0) == lax.broadcasted_iota(jnp.int32, (rows, rows), 1)
    return jnp.sum(jnp.where(eye, column, 0.0), axis=0, keepdims=True)


def spread_scale(scale, width):
    groups = scale.shape[0]
    spread = (
        lax.broadcasted_iota(jnp.int32, (groups, width), 1) // GROUP
        == lax.broadcasted_iota(jnp.int32, (groups, width), 0)
    ).astype(jnp.bfloat16)
    return lax.dot_general(
        scale, spread, (((0,), (0,)), ((), ())), preferred_element_type=jnp.float32
    )


def pack_kernel(groups, codes_hbm, exponents_hbm, clusters_hbm, message_ref, side_ref, codes_ref, exponents_ref, clusters_ref, sems):
    copies = [
        pltpu.make_async_copy(source, target, sems.at[i])
        for i, (source, target) in enumerate(
            [(exponents_hbm, exponents_ref), (clusters_hbm, clusters_ref), (codes_hbm, codes_ref)]
        )
    ]
    for copy in copies:
        copy.start()
    rows, width = codes_ref.shape
    copies[1].wait()
    code = clusters_ref[...] + 1
    row = lax.broadcasted_iota(jnp.int32, (SIDE_ROWS, rows), 0)
    side = jnp.where(row == 0, code >> 8, jnp.where(row == 1, code & 255, 0))
    side = side.astype(jnp.float32).astype(jnp.bfloat16)
    message_ref[rows:, 0:rows] = side
    message_ref[rows:, rows:] = jnp.zeros((SIDE_ROWS, width - rows), jnp.bfloat16)
    side_ref[groups:] = side
    copies[0].wait()
    scale = jnp.exp2(exponents_ref[...].astype(jnp.float32)).astype(jnp.bfloat16)
    side_ref[0:groups] = scale
    scale = spread_scale(scale, width)
    copies[2].wait()
    message_ref[0:rows] = (codes_ref[...].astype(jnp.float32) * scale).astype(jnp.bfloat16)


def cluster_code(parts):
    parts = parts.astype(jnp.float32)
    return parts[0:1] * 256.0 + parts[1:2]


def inverse_norm(values):
    wide = values.astype(jnp.float32)
    return lax.rsqrt(jnp.sum(wide * wide, axis=1, keepdims=True) + 1e-06)


def unpack_near(message_ref):
    rows = message_ref.shape[0] - SIDE_ROWS
    values = message_ref[0:rows]
    return values, inverse_norm(values), cluster_code(message_ref[rows:, 0:rows])


def unpack_far(codes_ref, side_ref):
    groups = side_ref.shape[0] - SIDE_ROWS
    scale = spread_scale(side_ref[0:groups], codes_ref.shape[1])
    values = (codes_ref[...].astype(jnp.float32) * scale).astype(jnp.bfloat16)
    return values, inverse_norm(values), cluster_code(side_ref[groups:])


def plane_kernel(planes, *refs):
    values_ref, lanes_ref, best_ref = refs[planes:]
    rows = refs[0].shape[0] - SIDE_ROWS
    best = jnp.full((1, rows), -1.0, jnp.float32)
    for r in range(planes):
        values, inverse, code = unpack_near(refs[r])
        values_ref[r * rows:(r + 1) * rows] = values
        inverse_row = flatten(inverse, rows)
        lanes_ref[0:1, r * rows:(r + 1) * rows] = code
        lanes_ref[1:2, r * rows:(r + 1) * rows] = inverse_row
        if r == 0:
            own, own_inverse, own_code = values, inverse_row, code
        dots = lax.dot_general(
            values, own, (((1,), (1,)), ((), ())), preferred_element_type=jnp.float32
        )
        same = expand(code, rows) == own_code
        if r == 0:
            same &= (
                lax.broadcasted_iota(jnp.int32, (rows, rows), 0)
                != lax.broadcasted_iota(jnp.int32, (rows, rows), 1)
            )
        scores = jnp.where(same, dots * inverse * own_inverse, -1.0)
        best = jnp.maximum(best, jnp.max(scores, axis=0, keepdims=True))
    best_ref[...] = jnp.full(best_ref.shape, -1.0, jnp.float32)
    best_ref[0:1, 0:rows] = best


def far_kernel(planes, fars, *refs):
    code_refs, side_refs = refs[:fars], refs[fars:2 * fars]
    values_ref, lanes_ref, before_ref = refs[2 * fars:2 * fars + 3]
    outs = refs[2 * fars + 3:]
    returned = max(fars - 1, 0)
    back_refs, best_refs = outs[:returned], outs[returned:]
    rows = code_refs[0].shape[0]
    bests = [before_ref[0:1, r * rows:(r + 1) * rows] for r in range(planes)]
    for i, (code_ref, side_ref) in enumerate(zip(code_refs, side_refs)):
        values, inverse, code = unpack_far(code_ref, side_ref)
        code = expand(code, rows)
        back = jnp.full((rows, 1), -1.0, jnp.float32)
        for r in range(planes):
            at = slice(r * rows, (r + 1) * rows)
            dots = lax.dot_general(
                values, values_ref[at], (((1,), (1,)), ((), ())),
                preferred_element_type=jnp.float32,
            )
            same = code == lanes_ref[0:1, at]
            scores = jnp.where(same, dots * inverse * lanes_ref[1:2, at], -1.0)
            if i < returned:
                back = jnp.maximum(back, jnp.max(scores, axis=1, keepdims=True))
            bests[r] = jnp.maximum(bests[r], jnp.max(scores, axis=0, keepdims=True))
        if i < returned:
            back_refs[i][...] = flatten(back, rows)
    for r in range(planes):
        best_refs[r][...] = bests[r]


def call(kernel, shapes, *operands):
    spec = pl.BlockSpec(memory_space=pltpu.VMEM)
    return pl.pallas_call(
        kernel,
        out_shape=[jax.ShapeDtypeStruct(shape, dtype) for shape, dtype in shapes],
        in_specs=[spec] * len(operands),
        out_specs=[spec] * len(shapes),
        compiler_params=pltpu.CompilerParams(vmem_limit_bytes=VMEM_LIMIT),
        cost_estimate=pl.CostEstimate(flops=COST, bytes_accessed=1, transcendentals=0),
    )(*operands)


def split_axis(count):
    planes = 1
    while planes * planes * 4 <= count:
        planes *= 2
    if count % planes or (count // planes) & (count // planes - 1):
        return 1, count
    return planes, count // planes


def far_rounds(height):
    rounds = []
    for step in range(2, height, 2):
        top = 1 << (step.bit_length() - 1)
        rounds.append([(a, a ^ step if a & top else a ^ (step + 1)) for a in range(height)])
    if height > 1:
        rounds.append([(a, a ^ 1) for a in range(height)])
    return rounds


def shards(codes, exponents, clusters):
    count = lax.axis_size("blk")
    rows, width = codes.shape
    groups = exponents.shape[1]
    plane, height = split_axis(count)
    near = [
        [(z * plane + p, z * plane + (p ^ r)) for z in range(height) for p in range(plane)]
        for r in range(plane)
    ]
    far = [
        [(a * plane + p, b * plane + p) for a, b in pairs for p in range(plane)]
        for pairs in far_rounds(height)
    ]
    backward = [[(b, a) for a, b in pairs] for pairs in far[:-1]]
    far_codes = [lax.ppermute(codes, "blk", pairs) for pairs in far]

    def near_phase(codes, exponents, clusters):
        message, side = pl.pallas_call(
            functools.partial(pack_kernel, groups),
            out_shape=[
                jax.ShapeDtypeStruct((rows + SIDE_ROWS, width), jnp.bfloat16),
                jax.ShapeDtypeStruct((groups + SIDE_ROWS, rows), jnp.bfloat16),
            ],
            in_specs=[pl.BlockSpec(memory_space=pl.ANY)] * 3,
            out_specs=[pl.BlockSpec(memory_space=pltpu.VMEM)] * 2,
            scratch_shapes=[
                pltpu.VMEM((rows, width), jnp.bfloat16),
                pltpu.VMEM((groups, rows), jnp.int32),
                pltpu.VMEM((1, rows), jnp.int32),
                pltpu.SemaphoreType.DMA((3,)),
            ],
            compiler_params=pltpu.CompilerParams(vmem_limit_bytes=PACK_LIMIT),
        )(codes, exponents, clusters)
        blocks = [message]
        for r in range(1, plane):
            relayed = r > 1 and r & 1
            blocks.append(
                lax.ppermute(blocks[r - 1], "blk", near[1]) if relayed
                else lax.ppermute(message, "blk", near[r])
            )
        if plane > 1:
            side, blocks[1] = lax.optimization_barrier((side, blocks[1]))
        sides = tuple(lax.ppermute(side, "blk", pairs) for pairs in far)
        values, lanes, best = call(
            functools.partial(plane_kernel, plane),
            [
                ((plane * rows, width), jnp.bfloat16),
                ((8, plane * rows), jnp.float32),
                ((1, plane * rows), jnp.float32),
            ],
            *blocks,
        )
        return values, sides, lanes, best

    values, far_sides, lanes, best = lax.cond(
        lax.axis_index("blk") >= 0,
        near_phase,
        lambda *operands: jax.tree.map(lambda t: jnp.zeros(t.shape, t.dtype), jax.eval_shape(near_phase, *operands)),
        codes, exponents.T, clusters[None],
    )
    outs = call(
        functools.partial(far_kernel, plane, len(far)),
        [((1, rows), jnp.float32)] * (plane + len(backward)),
        *far_codes, *far_sides, values, lanes, best,
    )
    backs, bests = outs[:len(backward)], outs[len(backward):]

    homes = [lax.ppermute(back, "blk", pairs) for pairs, back in zip(backward, backs)]
    homes += [lax.ppermute(bests[r], "blk", near[r]) for r in range(1, plane)]
    result = functools.reduce(jnp.maximum, homes, bests[0])
    return result.reshape(rows)


def solution(mesh):
    placed = (P(("parts", "blk"), None), P(("parts", "blk"), None), P(("parts", "blk")))
    return jax.shard_map(
        shards, mesh=mesh, in_specs=placed, out_specs=P(("parts", "blk")), check_vma=False
    )
```

```python
import functools
import jax
import jax.numpy as jnp
from jax import lax
from jax.experimental import pallas as pl
from jax.experimental.pallas import tpu as pltpu
from jax.sharding import PartitionSpec as P

GROUP = 32
SIDE_ROWS = 16
COST = 1
CHUNKS = 4
PACK_LIMIT = 32 * 1024 * 1024
VMEM_LIMIT = 32 * 1024 * 1024


def expand(lane_row, rows):
    eye = lax.broadcasted_iota(jnp.int32, (rows, rows), 0) == lax.broadcasted_iota(jnp.int32, (rows, rows), 1)
    return jnp.sum(jnp.where(eye, lane_row, 0.0), axis=1, keepdims=True)


def flatten(column, rows):
    eye = lax.broadcasted_iota(jnp.int32, (rows, rows), 0) == lax.broadcasted_iota(jnp.int32, (rows, rows), 1)
    return jnp.sum(jnp.where(eye, column, 0.0), axis=0, keepdims=True)


def spread_scale(scale, width):
    groups = scale.shape[0]
    spread = (
        lax.broadcasted_iota(jnp.int32, (groups, width), 1) // GROUP
        == lax.broadcasted_iota(jnp.int32, (groups, width), 0)
    ).astype(jnp.bfloat16)
    return lax.dot_general(
        scale, spread, (((0,), (0,)), ((), ())), preferred_element_type=jnp.float32
    )


def pack_kernel(groups, codes_hbm, exponents_hbm, clusters_hbm, message_ref, side_ref, codes_ref, exponents_ref, clusters_ref, sems):
    copies = [
        pltpu.make_async_copy(source, target, sems.at[i])
        for i, (source, target) in enumerate(
            [(exponents_hbm, exponents_ref), (clusters_hbm, clusters_ref), (codes_hbm, codes_ref)]
        )
    ]
    for copy in copies:
        copy.start()
    rows, width = codes_ref.shape
    copies[1].wait()
    code = clusters_ref[...] + 1
    row = lax.broadcasted_iota(jnp.int32, (SIDE_ROWS, rows), 0)
    side = jnp.where(row == 0, code >> 8, jnp.where(row == 1, code & 255, 0))
    side = side.astype(jnp.float32)
    message_ref[rows:, 0:rows] = side.astype(jnp.bfloat16)
    message_ref[rows:, rows:] = jnp.zeros((SIDE_ROWS, width - rows), jnp.bfloat16)
    copies[0].wait()
    scale = jnp.exp2(exponents_ref[...].astype(jnp.float32)).astype(jnp.bfloat16)
    side_ref[0:groups] = scale
    scale = spread_scale(scale, width)
    copies[2].wait()
    values = (codes_ref[...].astype(jnp.float32) * scale).astype(jnp.bfloat16)
    message_ref[0:rows] = values
    left = flatten(inverse_norm(values), rows)
    row = lax.broadcasted_iota(jnp.int32, (SIDE_ROWS, rows), 0)
    for i in range(2, 5):
        part = left.astype(jnp.bfloat16)
        left = left - part.astype(jnp.float32)
        side = jnp.where(row == i, part.astype(jnp.float32), side)
    side_ref[groups:] = side.astype(jnp.bfloat16)


def cluster_code(parts):
    parts = parts.astype(jnp.float32)
    return parts[0:1] * 256.0 + parts[1:2]


def inverse_norm(values):
    wide = values.astype(jnp.float32)
    return lax.rsqrt(jnp.sum(wide * wide, axis=1, keepdims=True) + 1e-06)


def unpack_near(message_ref):
    rows = message_ref.shape[0] - SIDE_ROWS
    values = message_ref[0:rows]
    return values, inverse_norm(values), cluster_code(message_ref[rows:, 0:rows])


def spread_kernel(groups, width, side_ref, scale_ref, column_ref):
    rows = side_ref.shape[1]
    scale_ref[...] = spread_scale(side_ref[0:groups], width).astype(jnp.bfloat16)
    parts = side_ref[groups:].astype(jnp.float32)
    column_ref[:, 0:1] = expand(cluster_code(parts), rows)
    column_ref[:, 1:2] = expand(parts[2:3] + parts[3:4] + parts[4:5], rows)


def plane_kernel(planes, *refs):
    values_ref, lanes_ref, best_ref = refs[planes:]
    rows = refs[0].shape[0] - SIDE_ROWS
    best = jnp.full((1, rows), -1.0, jnp.float32)
    for r in range(planes):
        values, inverse, code = unpack_near(refs[r])
        values_ref[r * rows:(r + 1) * rows] = values
        inverse_row = flatten(inverse, rows)
        lanes_ref[0:1, r * rows:(r + 1) * rows] = code
        lanes_ref[1:2, r * rows:(r + 1) * rows] = inverse_row
        if r == 0:
            own, own_inverse, own_code = values, inverse_row, code
        dots = lax.dot_general(
            values, own, (((1,), (1,)), ((), ())), preferred_element_type=jnp.float32
        )
        same = expand(code, rows) == own_code
        if r == 0:
            same &= (
                lax.broadcasted_iota(jnp.int32, (rows, rows), 0)
                != lax.broadcasted_iota(jnp.int32, (rows, rows), 1)
            )
        scores = jnp.where(same, dots * inverse * own_inverse, -1.0)
        best = jnp.maximum(best, jnp.max(scores, axis=0, keepdims=True))
    best_ref[...] = jnp.full(best_ref.shape, -1.0, jnp.float32)
    best_ref[0:1, 0:rows] = best


def far_kernel(planes, fars, *refs):
    code_refs, scale_refs, column_refs = refs[:fars], refs[fars:2 * fars], refs[2 * fars:3 * fars]
    values_ref, lanes_ref, before_ref = refs[3 * fars:3 * fars + 3]
    outs = refs[3 * fars + 3:]
    returned = max(fars - 1, 0)
    back_refs, best_refs = outs[:returned], outs[returned:]
    rows = code_refs[0].shape[0]
    bests = [before_ref[0:1, r * rows:(r + 1) * rows] for r in range(planes)]
    for i in range(fars):
        values = code_refs[i][...] * scale_refs[i][...]
        code, inverse = column_refs[i][:, 0:1], column_refs[i][:, 1:2]
        back = jnp.full((rows, rows), -1.0, jnp.float32)
        for r in range(planes):
            at = slice(r * rows, (r + 1) * rows)
            dots = lax.dot_general(
                values, values_ref[at], (((1,), (1,)), ((), ())),
                preferred_element_type=jnp.float32,
            )
            same = code == lanes_ref[0:1, at]
            scores = jnp.where(same, dots * inverse * lanes_ref[1:2, at], -1.0)
            if i < returned:
                back = jnp.maximum(back, scores)
            bests[r] = jnp.maximum(bests[r], jnp.max(scores, axis=0, keepdims=True))
        if i < returned:
            back_refs[i][...] = flatten(jnp.max(back, axis=1, keepdims=True), rows)
    for r in range(planes):
        best_refs[r][...] = bests[r]


def call(kernel, shapes, *operands):
    spec = pl.BlockSpec(memory_space=pltpu.VMEM)
    return pl.pallas_call(
        kernel,
        out_shape=[jax.ShapeDtypeStruct(shape, dtype) for shape, dtype in shapes],
        in_specs=[spec] * len(operands),
        out_specs=[spec] * len(shapes),
        compiler_params=pltpu.CompilerParams(vmem_limit_bytes=VMEM_LIMIT),
        cost_estimate=pl.CostEstimate(flops=COST, bytes_accessed=1, transcendentals=0),
    )(*operands)


def split_axis(count):
    planes = 1
    while planes * planes * 4 <= count:
        planes *= 2
    if count % planes or (count // planes) & (count // planes - 1):
        return 1, count
    return planes, count // planes


def far_rounds(height):
    rounds = []
    for step in range(2, height, 2):
        top = 1 << (step.bit_length() - 1)
        rounds.append([(a, a ^ step if a & top else a ^ (step + 1)) for a in range(height)])
    if height > 1:
        rounds.append([(a, a ^ 1) for a in range(height)])
    return rounds


def shards(codes, exponents, clusters):
    count = lax.axis_size("blk")
    rows, width = codes.shape
    groups = exponents.shape[1]
    plane, height = split_axis(count)
    near = [
        [(z * plane + p, z * plane + (p ^ r)) for z in range(height) for p in range(plane)]
        for r in range(plane)
    ]
    far = [
        [(a * plane + p, b * plane + p) for a, b in pairs for p in range(plane)]
        for pairs in far_rounds(height)
    ]
    backward = [[(b, a) for a, b in pairs] for pairs in far[:-1]]
    far_codes = [lax.ppermute(codes, "blk", pairs) for pairs in far]

    def near_phase(codes, exponents, clusters):
        message, side = pl.pallas_call(
            functools.partial(pack_kernel, groups),
            out_shape=[
                jax.ShapeDtypeStruct((rows + SIDE_ROWS, width), jnp.bfloat16),
                jax.ShapeDtypeStruct((groups + SIDE_ROWS, rows), jnp.bfloat16),
            ],
            in_specs=[pl.BlockSpec(memory_space=pl.ANY)] * 3,
            out_specs=[pl.BlockSpec(memory_space=pltpu.VMEM)] * 2,
            scratch_shapes=[
                pltpu.VMEM((rows, width), jnp.bfloat16),
                pltpu.VMEM((groups, rows), jnp.int32),
                pltpu.VMEM((1, rows), jnp.int32),
                pltpu.SemaphoreType.DMA((3,)),
            ],
            compiler_params=pltpu.CompilerParams(vmem_limit_bytes=PACK_LIMIT),
        )(codes, exponents, clusters)
        blocks = [message]
        for r in range(1, plane):
            relayed = r > 1 and r & 1
            blocks.append(
                lax.ppermute(blocks[r - 1], "blk", near[1]) if relayed
                else lax.ppermute(message, "blk", near[r])
            )
        if plane > 1:
            side, blocks[1] = lax.optimization_barrier((side, blocks[1]))
        sides = tuple(lax.ppermute(side, "blk", pairs) for pairs in far)
        values, lanes, best = call(
            functools.partial(plane_kernel, plane),
            [
                ((plane * rows, width), jnp.bfloat16),
                ((8, plane * rows), jnp.float32),
                ((1, plane * rows), jnp.float32),
            ],
            *blocks,
        )
        spreads = []
        for far_side in sides:
            if spreads:
                far_side, spreads[-1] = lax.optimization_barrier((far_side, spreads[-1]))
            else:
                far_side, best = lax.optimization_barrier((far_side, best))
            spreads.append(
                call(
                    functools.partial(spread_kernel, groups, width),
                    [((rows, width), jnp.bfloat16), ((rows, 128), jnp.float32)],
                    far_side,
                )
            )
        return values, [spread[0] for spread in spreads], [spread[1] for spread in spreads], lanes, best

    values, scales, columns, lanes, best = lax.cond(
        lax.axis_index("blk") >= 0,
        near_phase,
        lambda *operands: jax.tree.map(lambda t: jnp.zeros(t.shape, t.dtype), jax.eval_shape(near_phase, *operands)),
        codes, exponents.T, clusters[None],
    )
    outs = call(
        functools.partial(far_kernel, plane, len(far)),
        [((1, rows), jnp.float32)] * (plane + len(backward)),
        *far_codes, *scales, *columns, values, lanes, best,
    )
    backs, bests = outs[:len(backward)], outs[len(backward):]

    homes = [
        lax.ppermute(bests[r], "blk", near[r]) for r in [*range(2, plane), *range(1, min(plane, 2))]
    ]
    homes.append(bests[0])
    homes += [lax.ppermute(back, "blk", pairs) for pairs, back in zip(backward, backs)]
    result = functools.reduce(jnp.maximum, homes)
    return result.reshape(rows)


def solution(mesh):
    placed = (P(("parts", "blk"), None), P(("parts", "blk"), None), P(("parts", "blk")))
    return jax.shard_map(
        shards, mesh=mesh, in_specs=placed, out_specs=P(("parts", "blk")), check_vma=False
    )
```

```python
import functools
import jax
import jax.numpy as jnp
from jax import lax
from jax.experimental import pallas as pl
from jax.experimental.pallas import tpu as pltpu
from jax.sharding import PartitionSpec as P

GROUP = 32
SIDE_ROWS = 16
COST = 1
CHUNKS = 4
PACK_LIMIT = 32 * 1024 * 1024
VMEM_LIMIT = 32 * 1024 * 1024


def expand(lane_row, rows):
    eye = lax.broadcasted_iota(jnp.int32, (rows, rows), 0) == lax.broadcasted_iota(jnp.int32, (rows, rows), 1)
    return jnp.sum(jnp.where(eye, lane_row, 0.0), axis=1, keepdims=True)


def flatten(column, rows):
    eye = lax.broadcasted_iota(jnp.int32, (rows, rows), 0) == lax.broadcasted_iota(jnp.int32, (rows, rows), 1)
    return jnp.sum(jnp.where(eye, column, 0.0), axis=0, keepdims=True)


def spread_scale(scale, width):
    groups = scale.shape[0]
    spread = (
        lax.broadcasted_iota(jnp.int32, (groups, width), 1) // GROUP
        == lax.broadcasted_iota(jnp.int32, (groups, width), 0)
    ).astype(jnp.bfloat16)
    return lax.dot_general(
        scale, spread, (((0,), (0,)), ((), ())), preferred_element_type=jnp.float32
    )


def pack_kernel(groups, codes_hbm, exponents_hbm, clusters_hbm, message_ref, side_ref, codes_ref, exponents_ref, clusters_ref, sems):
    copies = [
        pltpu.make_async_copy(source, target, sems.at[i])
        for i, (source, target) in enumerate(
            [(exponents_hbm, exponents_ref), (clusters_hbm, clusters_ref), (codes_hbm, codes_ref)]
        )
    ]
    for copy in copies:
        copy.start()
    rows, width = codes_ref.shape
    copies[1].wait()
    code = clusters_ref[...] + 1
    row = lax.broadcasted_iota(jnp.int32, (SIDE_ROWS, rows), 0)
    side = jnp.where(row == 0, code >> 8, jnp.where(row == 1, code & 255, 0))
    side = side.astype(jnp.float32)
    message_ref[rows:, 0:rows] = side.astype(jnp.bfloat16)
    message_ref[rows:, rows:] = jnp.zeros((SIDE_ROWS, width - rows), jnp.bfloat16)
    copies[0].wait()
    scale = jnp.exp2(exponents_ref[...].astype(jnp.float32)).astype(jnp.bfloat16)
    side_ref[0:groups] = scale
    scale = spread_scale(scale, width)
    copies[2].wait()
    values = (codes_ref[...].astype(jnp.float32) * scale).astype(jnp.bfloat16)
    message_ref[0:rows] = values
    left = flatten(inverse_norm(values), rows)
    row = lax.broadcasted_iota(jnp.int32, (SIDE_ROWS, rows), 0)
    for i in range(2, 5):
        part = left.astype(jnp.bfloat16)
        left = left - part.astype(jnp.float32)
        side = jnp.where(row == i, part.astype(jnp.float32), side)
    side_ref[groups:] = side.astype(jnp.bfloat16)


def cluster_code(parts):
    parts = parts.astype(jnp.float32)
    return parts[0:1] * 256.0 + parts[1:2]


def inverse_norm(values):
    wide = values.astype(jnp.float32)
    return lax.rsqrt(jnp.sum(wide * wide, axis=1, keepdims=True) + 1e-06)


def unpack_near(message_ref):
    rows = message_ref.shape[0] - SIDE_ROWS
    values = message_ref[0:rows]
    return values, inverse_norm(values), cluster_code(message_ref[rows:, 0:rows])


def spread_kernel(groups, width, side_ref, scale_ref, column_ref):
    rows = side_ref.shape[1]
    scale_ref[...] = spread_scale(side_ref[0:groups], width).astype(jnp.bfloat16)
    parts = side_ref[groups:].astype(jnp.float32)
    column_ref[:, 0:1] = expand(cluster_code(parts), rows)
    column_ref[:, 1:2] = expand(parts[2:3] + parts[3:4] + parts[4:5], rows)


def plane_kernel(planes, *refs):
    values_ref, lanes_ref, best_ref = refs[planes:]
    rows = refs[0].shape[0] - SIDE_ROWS
    best = jnp.full((1, rows), -1.0, jnp.float32)
    for r in range(planes):
        values, inverse, code = unpack_near(refs[r])
        values_ref[r * rows:(r + 1) * rows] = values
        inverse_row = flatten(inverse, rows)
        lanes_ref[0:1, r * rows:(r + 1) * rows] = code
        lanes_ref[1:2, r * rows:(r + 1) * rows] = inverse_row
        if r == 0:
            own, own_inverse, own_code = values, inverse_row, code
        dots = lax.dot_general(
            values, own, (((1,), (1,)), ((), ())), preferred_element_type=jnp.float32
        )
        same = expand(code, rows) == own_code
        if r == 0:
            same &= (
                lax.broadcasted_iota(jnp.int32, (rows, rows), 0)
                != lax.broadcasted_iota(jnp.int32, (rows, rows), 1)
            )
        scores = jnp.where(same, dots * inverse * own_inverse, -1.0)
        best = jnp.maximum(best, jnp.max(scores, axis=0, keepdims=True))
    best_ref[...] = jnp.full(best_ref.shape, -1.0, jnp.float32)
    best_ref[0:1, 0:rows] = best


def swap_kernel(planes, code_ref, scale_ref, column_ref, values_ref, lanes_ref, before_ref, best_ref):
    rows = code_ref.shape[0]
    values = code_ref[...] * scale_ref[...]
    code, inverse = column_ref[:, 0:1], column_ref[:, 1:2]
    for r in range(planes):
        at = slice(r * rows, (r + 1) * rows)
        dots = lax.dot_general(
            values, values_ref[at], (((1,), (1,)), ((), ())),
            preferred_element_type=jnp.float32,
        )
        same = code == lanes_ref[0:1, at]
        scores = jnp.where(same, dots * inverse * lanes_ref[1:2, at], -1.0)
        best_ref[0:1, at] = jnp.maximum(before_ref[0:1, at], jnp.max(scores, axis=0, keepdims=True))


def far_kernel(planes, fars, *refs):
    code_refs, scale_refs, column_refs = refs[:fars], refs[fars:2 * fars], refs[2 * fars:3 * fars]
    values_ref, lanes_ref, before_ref = refs[3 * fars:3 * fars + 3]
    outs = refs[3 * fars + 3:]
    returned = fars
    back_refs, best_refs = outs[:returned], outs[returned:]
    rows = code_refs[0].shape[0]
    bests = [before_ref[0:1, r * rows:(r + 1) * rows] for r in range(planes)]
    for i in range(fars):
        values = code_refs[i][...] * scale_refs[i][...]
        code, inverse = column_refs[i][:, 0:1], column_refs[i][:, 1:2]
        back = jnp.full((rows, rows), -1.0, jnp.float32)
        for r in range(planes):
            at = slice(r * rows, (r + 1) * rows)
            dots = lax.dot_general(
                values, values_ref[at], (((1,), (1,)), ((), ())),
                preferred_element_type=jnp.float32,
            )
            same = code == lanes_ref[0:1, at]
            scores = jnp.where(same, dots * inverse * lanes_ref[1:2, at], -1.0)
            back = jnp.maximum(back, scores)
            bests[r] = jnp.maximum(bests[r], jnp.max(scores, axis=0, keepdims=True))
        back_refs[i][...] = flatten(jnp.max(back, axis=1, keepdims=True), rows)
    cross_refs, even_refs = best_refs[:1], best_refs[min(planes - 1, 1):]
    for r in range(planes):
        if r % 2 == 0:
            even_refs[r // 2][...] = bests[r]
        else:
            cross_refs[0][r // 2:r // 2 + 1] = bests[r]


def call(kernel, shapes, *operands):
    spec = pl.BlockSpec(memory_space=pltpu.VMEM)
    return pl.pallas_call(
        kernel,
        out_shape=[jax.ShapeDtypeStruct(shape, dtype) for shape, dtype in shapes],
        in_specs=[spec] * len(operands),
        out_specs=[spec] * len(shapes),
        compiler_params=pltpu.CompilerParams(vmem_limit_bytes=VMEM_LIMIT),
        cost_estimate=pl.CostEstimate(flops=COST, bytes_accessed=1, transcendentals=0),
    )(*operands)


def split_axis(count):
    planes = 1
    while planes * planes * 4 <= count:
        planes *= 2
    if count % planes or (count // planes) & (count // planes - 1):
        return 1, count
    return planes, count // planes


def far_rounds(height):
    rounds = []
    for step in range(2, height, 2):
        top = 1 << (step.bit_length() - 1)
        rounds.append([(a, a ^ step if a & top else a ^ (step + 1)) for a in range(height)])
    if height > 1:
        rounds.insert(0, [(a, a ^ 1) for a in range(height)])
    return rounds


def shards(codes, exponents, clusters):
    count = lax.axis_size("blk")
    rows, width = codes.shape
    groups = exponents.shape[1]
    plane, height = split_axis(count)
    near = [
        [(z * plane + p, z * plane + (p ^ r)) for z in range(height) for p in range(plane)]
        for r in range(plane)
    ]
    far = [
        [(a * plane + p, b * plane + p) for a, b in pairs for p in range(plane)]
        for pairs in far_rounds(height)
    ]
    backward = [[(b, a) for a, b in pairs] for pairs in far[1:]]
    far_codes = [lax.ppermute(codes, "blk", pairs) for pairs in far]

    message, side = pl.pallas_call(
        functools.partial(pack_kernel, groups),
        out_shape=[
            jax.ShapeDtypeStruct((rows + SIDE_ROWS, width), jnp.bfloat16),
            jax.ShapeDtypeStruct((groups + SIDE_ROWS, rows), jnp.bfloat16),
        ],
        in_specs=[pl.BlockSpec(memory_space=pl.ANY)] * 3,
        out_specs=[pl.BlockSpec(memory_space=pltpu.VMEM)] * 2,
        scratch_shapes=[
            pltpu.VMEM((rows, width), jnp.bfloat16),
            pltpu.VMEM((groups, rows), jnp.int32),
            pltpu.VMEM((1, rows), jnp.int32),
            pltpu.SemaphoreType.DMA((3,)),
        ],
        compiler_params=pltpu.CompilerParams(vmem_limit_bytes=PACK_LIMIT),
    )(codes, exponents.T, clusters[None])
    far_sides = [lax.ppermute(side, "blk", pairs) for pairs in far[1:]]

    def near_phase(message, side):
        blocks = [message]
        for r in range(1, plane):
            relayed = r > 1 and r & 1
            blocks.append(
                lax.ppermute(blocks[r - 1], "blk", near[1]) if relayed
                else lax.ppermute(message, "blk", near[r])
            )
        if plane > 1:
            side, blocks[1] = lax.optimization_barrier((side, blocks[1]))
        sides = tuple(lax.ppermute(side, "blk", pairs) for pairs in far[:1])
        values, lanes, best = call(
            functools.partial(plane_kernel, plane),
            [
                ((plane * rows, width), jnp.bfloat16),
                ((8, plane * rows), jnp.float32),
                ((1, plane * rows), jnp.float32),
            ],
            *blocks,
        )
        spreads = []
        for far_side in sides:
            if spreads:
                far_side, spreads[-1] = lax.optimization_barrier((far_side, spreads[-1]))
            else:
                far_side, best = lax.optimization_barrier((far_side, best))
            spreads.append(
                call(
                    functools.partial(spread_kernel, groups, width),
                    [((rows, width), jnp.bfloat16), ((rows, 128), jnp.float32)],
                    far_side,
                )
            )
        return values, [spread[0] for spread in spreads], [spread[1] for spread in spreads], lanes, best

    values, scales, columns, lanes, best = lax.cond(
        lax.axis_index("blk") >= 0,
        near_phase,
        lambda *operands: jax.tree.map(lambda t: jnp.zeros(t.shape, t.dtype), jax.eval_shape(near_phase, *operands)),
        message, side,
    )
    for block in zip(far_codes, scales, columns):
        (best,) = call(
            functools.partial(swap_kernel, plane),
            [((1, plane * rows), jnp.float32)],
            *block, values, lanes, best,
        )
    spreads = []
    for far_side in far_sides:
        far_side, best = lax.optimization_barrier((far_side, best))
        spreads.append(
            call(
                functools.partial(spread_kernel, groups, width),
                [((rows, width), jnp.bfloat16), ((rows, 128), jnp.float32)],
                far_side,
            )
        )
    halves = plane // 2
    outs = call(
        functools.partial(far_kernel, plane, len(backward)),
        [((1, rows), jnp.float32)] * len(backward)
        + [((halves, rows), jnp.float32)] * min(halves, 1)
        + [((1, rows), jnp.float32)] * (plane - halves),
        *far_codes[1:], *[spread[0] for spread in spreads], *[spread[1] for spread in spreads],
        values, lanes, best,
    )
    backs, bests = outs[:len(backward)], outs[len(backward):]

    if halves:
        crossed = lax.ppermute(bests[0], "blk", near[1])
        bests = [jnp.maximum(own, crossed[i:i + 1]) for i, own in enumerate(bests[1:])]
    homes = [lax.ppermute(bests[i], "blk", near[2 * i]) for i in range(1, len(bests))]
    homes = [lax.ppermute(back, "blk", pairs) for pairs, back in zip(backward, backs)] + homes + [bests[0]]
    result = functools.reduce(jnp.maximum, homes)
    return result.reshape(rows)


def solution(mesh):
    placed = (P(("parts", "blk"), None), P(("parts", "blk"), None), P(("parts", "blk")))
    return jax.shard_map(
        shards, mesh=mesh, in_specs=placed, out_specs=P(("parts", "blk")), check_vma=False
    )
```

```python
import functools
import jax
import jax.numpy as jnp
from jax import lax
from jax.experimental import pallas as pl
from jax.experimental.pallas import tpu as pltpu
from jax.sharding import PartitionSpec as P

GROUP = 32
SIDE_ROWS = 16
COST = 1
CHUNKS = 4
PACK_LIMIT = 32 * 1024 * 1024
VMEM_LIMIT = 32 * 1024 * 1024


def expand(lane_row, rows):
    eye = lax.broadcasted_iota(jnp.int32, (rows, rows), 0) == lax.broadcasted_iota(jnp.int32, (rows, rows), 1)
    return jnp.sum(jnp.where(eye, lane_row, 0.0), axis=1, keepdims=True)


def flatten(column, rows):
    eye = lax.broadcasted_iota(jnp.int32, (rows, rows), 0) == lax.broadcasted_iota(jnp.int32, (rows, rows), 1)
    return jnp.sum(jnp.where(eye, column, 0.0), axis=0, keepdims=True)


def spread_scale(scale, width):
    groups = scale.shape[0]
    spread = (
        lax.broadcasted_iota(jnp.int32, (groups, width), 1) // GROUP
        == lax.broadcasted_iota(jnp.int32, (groups, width), 0)
    ).astype(jnp.bfloat16)
    return lax.dot_general(
        scale, spread, (((0,), (0,)), ((), ())), preferred_element_type=jnp.float32
    )


def pack_kernel(groups, codes_hbm, exponents_hbm, clusters_hbm, message_ref, side_ref, codes_ref, exponents_ref, clusters_ref, sems):
    copies = [
        pltpu.make_async_copy(source, target, sems.at[i])
        for i, (source, target) in enumerate(
            [(exponents_hbm, exponents_ref), (clusters_hbm, clusters_ref), (codes_hbm, codes_ref)]
        )
    ]
    for copy in copies:
        copy.start()
    rows, width = codes_ref.shape
    copies[1].wait()
    code = clusters_ref[...] + 1
    row = lax.broadcasted_iota(jnp.int32, (SIDE_ROWS, rows), 0)
    side = jnp.where(row == 0, code >> 8, jnp.where(row == 1, code & 255, 0))
    side = side.astype(jnp.float32)
    message_ref[rows:, 0:rows] = side.astype(jnp.bfloat16)
    message_ref[rows:, rows:] = jnp.zeros((SIDE_ROWS, width - rows), jnp.bfloat16)
    copies[0].wait()
    scale = jnp.exp2(exponents_ref[...].astype(jnp.float32)).astype(jnp.bfloat16)
    side_ref[0:groups] = scale
    scale = spread_scale(scale, width)
    copies[2].wait()
    values = (codes_ref[...].astype(jnp.float32) * scale).astype(jnp.bfloat16)
    message_ref[0:rows] = values
    left = flatten(inverse_norm(values), rows)
    row = lax.broadcasted_iota(jnp.int32, (SIDE_ROWS, rows), 0)
    for i in range(2, 5):
        part = left.astype(jnp.bfloat16)
        left = left - part.astype(jnp.float32)
        side = jnp.where(row == i, part.astype(jnp.float32), side)
    side_ref[groups:] = side.astype(jnp.bfloat16)


def cluster_code(parts):
    parts = parts.astype(jnp.float32)
    return parts[0:1] * 256.0 + parts[1:2]


def inverse_norm(values):
    wide = values.astype(jnp.float32)
    return lax.rsqrt(jnp.sum(wide * wide, axis=1, keepdims=True) + 1e-06)


def unpack_near(message_ref):
    rows = message_ref.shape[0] - SIDE_ROWS
    values = message_ref[0:rows]
    return values, inverse_norm(values), cluster_code(message_ref[rows:, 0:rows])


def spread_kernel(groups, width, side_ref, scale_ref, column_ref):
    rows = side_ref.shape[1]
    scale_ref[...] = spread_scale(side_ref[0:groups], width).astype(jnp.bfloat16)
    parts = side_ref[groups:].astype(jnp.float32)
    column_ref[:, 0:1] = expand(cluster_code(parts), rows)
    column_ref[:, 1:2] = expand(parts[2:3] + parts[3:4] + parts[4:5], rows)


def plane_kernel(planes, *refs):
    values_ref, lanes_ref, best_ref = refs[planes:]
    rows = refs[0].shape[0] - SIDE_ROWS
    best = jnp.full((1, rows), -1.0, jnp.float32)
    for r in range(planes):
        values, inverse, code = unpack_near(refs[r])
        values_ref[r * rows:(r + 1) * rows] = values
        inverse_row = flatten(inverse, rows)
        lanes_ref[0:1, r * rows:(r + 1) * rows] = code
        lanes_ref[1:2, r * rows:(r + 1) * rows] = inverse_row
        if r == 0:
            own, own_inverse, own_code = values, inverse_row, code
        dots = lax.dot_general(
            values, own, (((1,), (1,)), ((), ())), preferred_element_type=jnp.float32
        )
        same = expand(code, rows) == own_code
        if r == 0:
            same &= (
                lax.broadcasted_iota(jnp.int32, (rows, rows), 0)
                != lax.broadcasted_iota(jnp.int32, (rows, rows), 1)
            )
        scores = jnp.where(same, dots * inverse * own_inverse, -1.0)
        best = jnp.maximum(best, jnp.max(scores, axis=0, keepdims=True))
    best_ref[...] = jnp.full(best_ref.shape, -1.0, jnp.float32)
    best_ref[0:1, 0:rows] = best


def swap_kernel(planes, code_ref, scale_ref, column_ref, values_ref, lanes_ref, before_ref, best_ref):
    rows = code_ref.shape[0]
    values = code_ref[...] * scale_ref[...]
    code, inverse = column_ref[:, 0:1], column_ref[:, 1:2]
    for r in range(planes):
        at = slice(r * rows, (r + 1) * rows)
        dots = lax.dot_general(
            values, values_ref[at], (((1,), (1,)), ((), ())),
            preferred_element_type=jnp.float32,
        )
        same = code == lanes_ref[0:1, at]
        scores = jnp.where(same, dots * inverse * lanes_ref[1:2, at], -1.0)
        best_ref[0:1, at] = jnp.maximum(before_ref[0:1, at], jnp.max(scores, axis=0, keepdims=True))


def far_kernel(planes, fars, *refs):
    code_refs, side_refs = refs[:fars], refs[fars:2 * fars]
    values_ref, lanes_ref, before_ref = refs[2 * fars:2 * fars + 3]
    outs = refs[2 * fars + 3:]
    groups = side_refs[0].shape[0] - SIDE_ROWS if fars else 0
    returned = fars
    back_refs, best_refs = outs[:returned], outs[returned:]
    rows = code_refs[0].shape[0]
    bests = [before_ref[0:1, r * rows:(r + 1) * rows] for r in range(planes)]
    for i in range(fars):
        scale = spread_scale(side_refs[i][0:groups], code_refs[i].shape[1])
        values = code_refs[i][...] * scale.astype(jnp.bfloat16)
        parts = side_refs[i][groups:].astype(jnp.float32)
        code = expand(cluster_code(parts), rows)
        inverse = expand(parts[2:3] + parts[3:4] + parts[4:5], rows)
        back = jnp.full((rows, rows), -1.0, jnp.float32)
        for r in range(planes):
            at = slice(r * rows, (r + 1) * rows)
            dots = lax.dot_general(
                values, values_ref[at], (((1,), (1,)), ((), ())),
                preferred_element_type=jnp.float32,
            )
            same = code == lanes_ref[0:1, at]
            scores = jnp.where(same, dots * inverse * lanes_ref[1:2, at], -1.0)
            back = jnp.maximum(back, scores)
            bests[r] = jnp.maximum(bests[r], jnp.max(scores, axis=0, keepdims=True))
        back_refs[i][...] = flatten(jnp.max(back, axis=1, keepdims=True), rows)
    cross_refs, even_refs = best_refs[:1], best_refs[min(planes - 1, 1):]
    for r in range(planes):
        if r % 2 == 0:
            even_refs[r // 2][...] = bests[r]
        else:
            cross_refs[0][r // 2:r // 2 + 1] = bests[r]


def call(kernel, shapes, *operands):
    spec = pl.BlockSpec(memory_space=pltpu.VMEM)
    return pl.pallas_call(
        kernel,
        out_shape=[jax.ShapeDtypeStruct(shape, dtype) for shape, dtype in shapes],
        in_specs=[spec] * len(operands),
        out_specs=[spec] * len(shapes),
        compiler_params=pltpu.CompilerParams(vmem_limit_bytes=VMEM_LIMIT),
        cost_estimate=pl.CostEstimate(flops=COST, bytes_accessed=1, transcendentals=0),
    )(*operands)


def split_axis(count):
    planes = 1
    while planes * planes * 4 <= count:
        planes *= 2
    if count % planes or (count // planes) & (count // planes - 1):
        return 1, count
    return planes, count // planes


def far_rounds(height):
    rounds = []
    for step in range(2, height, 2):
        top = 1 << (step.bit_length() - 1)
        rounds.append([(a, a ^ step if a & top else a ^ (step + 1)) for a in range(height)])
    if height > 1:
        rounds.insert(0, [(a, a ^ 1) for a in range(height)])
    return rounds


def shards(codes, exponents, clusters):
    count = lax.axis_size("blk")
    rows, width = codes.shape
    groups = exponents.shape[1]
    plane, height = split_axis(count)
    near = [
        [(z * plane + p, z * plane + (p ^ r)) for z in range(height) for p in range(plane)]
        for r in range(plane)
    ]
    far = [
        [(a * plane + p, b * plane + p) for a, b in pairs for p in range(plane)]
        for pairs in far_rounds(height)
    ]
    backward = [[(b, a) for a, b in pairs] for pairs in far[1:]]
    far_codes = [lax.ppermute(codes, "blk", pairs) for pairs in far]

    message, side = pl.pallas_call(
        functools.partial(pack_kernel, groups),
        out_shape=[
            jax.ShapeDtypeStruct((rows + SIDE_ROWS, width), jnp.bfloat16),
            jax.ShapeDtypeStruct((groups + SIDE_ROWS, rows), jnp.bfloat16),
        ],
        in_specs=[pl.BlockSpec(memory_space=pl.ANY)] * 3,
        out_specs=[pl.BlockSpec(memory_space=pltpu.VMEM)] * 2,
        scratch_shapes=[
            pltpu.VMEM((rows, width), jnp.bfloat16),
            pltpu.VMEM((groups, rows), jnp.int32),
            pltpu.VMEM((1, rows), jnp.int32),
            pltpu.SemaphoreType.DMA((3,)),
        ],
        compiler_params=pltpu.CompilerParams(vmem_limit_bytes=PACK_LIMIT),
    )(codes, exponents.T, clusters[None])
    far_sides = [lax.ppermute(side, "blk", pairs) for pairs in far[1:]]

    def near_phase(message, side):
        blocks = [message]
        for r in range(1, plane):
            relayed = r > 1 and r & 1
            blocks.append(
                lax.ppermute(blocks[r - 1], "blk", near[1]) if relayed
                else lax.ppermute(message, "blk", near[r])
            )
        if plane > 1:
            side, blocks[1] = lax.optimization_barrier((side, blocks[1]))
        sides = tuple(lax.ppermute(side, "blk", pairs) for pairs in far[:1])
        values, lanes, best = call(
            functools.partial(plane_kernel, plane),
            [
                ((plane * rows, width), jnp.bfloat16),
                ((8, plane * rows), jnp.float32),
                ((1, plane * rows), jnp.float32),
            ],
            *blocks,
        )
        spreads = []
        for far_side in sides:
            if spreads:
                far_side, spreads[-1] = lax.optimization_barrier((far_side, spreads[-1]))
            else:
                far_side, best = lax.optimization_barrier((far_side, best))
            spreads.append(
                call(
                    functools.partial(spread_kernel, groups, width),
                    [((rows, width), jnp.bfloat16), ((rows, 128), jnp.float32)],
                    far_side,
                )
            )
        return values, [spread[0] for spread in spreads], [spread[1] for spread in spreads], lanes, best

    values, scales, columns, lanes, best = lax.cond(
        lax.axis_index("blk") >= 0,
        near_phase,
        lambda *operands: jax.tree.map(lambda t: jnp.zeros(t.shape, t.dtype), jax.eval_shape(near_phase, *operands)),
        message, side,
    )
    for block in zip(far_codes, scales, columns):
        (best,) = call(
            functools.partial(swap_kernel, plane),
            [((1, plane * rows), jnp.float32)],
            *block, values, lanes, best,
        )
    if far_sides:
        *far_sides, best = lax.optimization_barrier((*far_sides, best))
    halves = plane // 2
    outs = call(
        functools.partial(far_kernel, plane, len(backward)),
        [((1, rows), jnp.float32)] * len(backward)
        + [((halves, rows), jnp.float32)] * min(halves, 1)
        + [((1, rows), jnp.float32)] * (plane - halves),
        *far_codes[1:], *far_sides, values, lanes, best,
    )
    backs, bests = outs[:len(backward)], outs[len(backward):]

    if halves:
        crossed = lax.ppermute(bests[0], "blk", near[1])
        bests = [jnp.maximum(own, crossed[i:i + 1]) for i, own in enumerate(bests[1:])]
    homes = [lax.ppermute(bests[i], "blk", near[2 * i]) for i in range(1, len(bests))]
    homes = [lax.ppermute(back, "blk", pairs) for pairs, back in zip(backward, backs)] + homes + [bests[0]]
    result = functools.reduce(jnp.maximum, homes)
    return result.reshape(rows)


def solution(mesh):
    placed = (P(("parts", "blk"), None), P(("parts", "blk"), None), P(("parts", "blk")))
    return jax.shard_map(
        shards, mesh=mesh, in_specs=placed, out_specs=P(("parts", "blk")), check_vma=False
    )
```
